32 devices in a mesh: blk: 16 (over z, y, core), pair: 2 (over x).
Axes of the slice: x: 2, y: 2, z: 4, core: 2. Of those that a mesh axis runs over, the one named last changes fastest.
Arguments:
- particles: float32 [32768, 512], P(('blk', 'pair'))
- log_prior: float32 [32768], P(('blk', 'pair'))
- transition: bfloat16 [512, 512], replicated, may hold values from -0.25 to 0.25
- drive_vector: float32 [512], replicated, may hold values from -3 to 3
- current: float32 [4], replicated, may hold values from -4 to 4
- decay_rate: float32 [512], replicated, may hold values from 0.3 to 0.98
- obs_matrix: bfloat16 [512, 128], replicated, may hold values from -0.25 to 0.25
- obs_weight: float32 [128], replicated, may hold values from 0.05 to 0.5
- observed: float32 [4, 128], replicated
- ancestors: int32 [32768], P(('blk', 'pair')), may hold values from 0 to 1023
- cycle_pick: int32 [8192], P(('blk', 'pair')), may hold values from 0 to 1023, as said below
- pair_pick: int32 [1024], P(('blk', 'pair')), may hold values from 0 to 1023, as said below
Outputs:
- migrated: float32 [32768, 512], P(('blk', 'pair'))
- group_logw: float32 [32768], P(('blk', 'pair'))
- mean_state: float32 [512], replicated
The draws below stay inside these ranges and needn't reach their ends.
Inputs may be any that keep to these rules, and one draw needn't show every extreme that they name: On each device, cycle_pick's 256 entries and pair_pick's 32 entries are distinct local positions, none shared between the two. `pair_pick`: distinct local positions, none in the same device's cycle_pick.
All inputs are finite; a program needn't handle non-finite values.
Results may differ from the reference program's by a relative error of at most 0.013.
Values sent between devices are 32-bit elements; how exact they have to be, the bound alone decides.
A program may use at most 64 MiB of HBM per device.

```python
import math
import jax
import jax.numpy as jnp
from jax import lax

S = 512
OBS = 128
PART_DEV = 1024
STEPS = 4
CYCLE_ROWS = 256
PAIR_ROWS = 32
PARTICLES = 32768
N_BLK = 16
N_PAIR = 2
DEVICES = 32


def draw_particles(key, part):
    common = jax.random.normal(jax.random.fold_in(key, 1), (S,), jnp.float32)
    spread = jax.random.normal(jax.random.fold_in(key, 2), (PARTICLES, S), jnp.float32)
    return common + 0.5 * spread


def draw_log_prior(key, part):
    ramp = 5.0 * jnp.arange(PARTICLES, dtype=jnp.float32) / PARTICLES
    return ramp + 0.5 * jax.random.normal(key, (PARTICLES,), jnp.float32)


def draw_observed(key, part):
    values = jax.random.normal(key, (STEPS, OBS), jnp.float32)
    return values


def pick_tables(key):
    base = jax.random.fold_in(key, 77)
    keys = jax.random.split(base, DEVICES)
    orders = jax.vmap(lambda one_key: jax.random.permutation(one_key, PART_DEV))(keys)
    return orders.astype(jnp.int32)


def draw_cycle_pick(key, part):
    orders = pick_tables(key)
    return orders[:, :CYCLE_ROWS].reshape(-1)


def draw_pair_pick(key, part):
    orders = pick_tables(key)
    return orders[:, CYCLE_ROWS:CYCLE_ROWS + PAIR_ROWS].reshape(-1)


def with_ends(result, stream_key, low, high):
    shape = result.shape
    place = [jax.random.randint(jax.random.fold_in(stream_key, axis), (), 0, shape[axis]) for axis in range(len(shape))]
    result = result.at[tuple(place)].set(low)
    longest = shape.index(max(shape))
    place[longest] = (place[longest] + 1) % shape[longest]
    return result.at[tuple(place)].set(high)


def centred(stream_key, extent, scale, limit, kind=jnp.bfloat16):
    result = jax.random.normal(stream_key, extent, jnp.float32) * scale
    return jnp.minimum(jnp.maximum(result, -limit), limit).astype(kind)


def setup_inputs(seed: int = 0) -> dict:
    splits = jax.random.split(jax.random.key(seed), 13)
    particles = draw_particles(jax.random.fold_in(splits[12], 71), 0)
    log_prior = draw_log_prior(jax.random.fold_in(splits[12], 71), 0)
    transition = centred(splits[2], (S, S), S ** -0.5, 0.25)
    drive_vector = centred(splits[3], (S,), 0.5, 3.0, jnp.float32)
    current = centred(splits[4], (STEPS,), 1.0, 4.0, jnp.float32)
    decay_rate = jnp.clip(jnp.exp(jax.random.uniform(splits[5], (S,), jnp.float32, math.log(0.3), math.log(0.98))), 0.3, 0.98)
    obs_matrix = centred(splits[6], (S, OBS), S ** -0.5, 0.25)
    obs_weight = jnp.clip(jnp.exp(jax.random.uniform(splits[7], (OBS,), jnp.float32, math.log(0.05), math.log(0.5))), 0.05, 0.5)
    observed = draw_observed(jax.random.fold_in(splits[12], 71), 0)
    ancestors = with_ends(jax.random.randint(splits[9], (PARTICLES,), 0, PART_DEV), jax.random.fold_in(splits[9], 1), 0, PART_DEV - 1).astype(jnp.int32)
    cycle_pick = draw_cycle_pick(jax.random.fold_in(splits[12], 71), 0)
    pair_pick = draw_pair_pick(jax.random.fold_in(splits[12], 71), 0)
    return {"particles": particles, "log_prior": log_prior, "transition": transition, "drive_vector": drive_vector, "current": current, "decay_rate": decay_rate, "obs_matrix": obs_matrix, "obs_weight": obs_weight, "observed": observed, "ancestors": ancestors, "cycle_pick": cycle_pick, "pair_pick": pair_pick}


def place_rows(base_rows, cycle_pos, cycle_in, pair_pos, pair_in):
    return base_rows.at[cycle_pos].set(cycle_in).at[pair_pos].set(pair_in)


def reference(particles, log_prior, transition, drive_vector, current, decay_rate, obs_matrix, obs_weight, observed, ancestors, cycle_pick, pair_pick):
    state = particles
    logw = log_prior
    rounded = state.astype(jnp.bfloat16)
    for step_index in range(STEPS):
        drift = jnp.dot(rounded, transition, preferred_element_type=jnp.float32) + current[step_index] * drive_vector
        state = decay_rate * state + jnp.tanh(drift)
        rounded = state.astype(jnp.bfloat16)
        predicted = jnp.dot(rounded, obs_matrix, preferred_element_type=jnp.float32)
        misfit = predicted - observed[step_index]
        logw = logw - 0.5 * jnp.sum(obs_weight * misfit * misfit, axis=1)
    peak = jnp.max(logw)
    expw = jnp.exp(logw - peak)
    total = jnp.sum(expw)
    mean_state = jnp.dot(expw, state, precision=lax.Precision.HIGHEST) / total
    groups = N_BLK * N_PAIR
    dev_sum = jnp.sum(expw.reshape(groups, PART_DEV), axis=1)
    dev_logw = jnp.log(jnp.maximum(groups * dev_sum / total, 0.1))
    states = state.reshape(groups, PART_DEV, S)
    parents = ancestors.reshape(groups, PART_DEV).astype(jnp.int32)
    resampled = jnp.take_along_axis(states, parents[:, :, None], axis=1)
    cycle_pos = cycle_pick.reshape(groups, CYCLE_ROWS)
    pair_pos = pair_pick.reshape(groups, PAIR_ROWS)
    cycle_sent = jnp.take_along_axis(resampled, cycle_pos[:, :, None], axis=1)
    pair_sent = jnp.take_along_axis(resampled, pair_pos[:, :, None], axis=1)
    cycle_in = jnp.roll(cycle_sent.reshape(N_BLK, N_PAIR, CYCLE_ROWS, S), 1, axis=0).reshape(groups, CYCLE_ROWS, S)
    grid_logw = dev_logw.reshape(N_BLK, N_PAIR)
    cycle_w = jnp.roll(grid_logw, 1, axis=0).reshape(groups)
    half_pair = N_PAIR // 2
    pair_in = jnp.roll(pair_sent.reshape(N_BLK, N_PAIR, PAIR_ROWS, S), half_pair, axis=1).reshape(groups, PAIR_ROWS, S)
    pair_w = jnp.roll(grid_logw, half_pair, axis=1).reshape(groups)
    migrated = jax.vmap(place_rows)(resampled, cycle_pos, cycle_in, pair_pos, pair_in)
    base_w = jnp.broadcast_to(dev_logw[:, None], (groups, PART_DEV))
    cycle_wrows = jnp.broadcast_to(cycle_w[:, None], (groups, CYCLE_ROWS))
    pair_wrows = jnp.broadcast_to(pair_w[:, None], (groups, PAIR_ROWS))
    group_logw = jax.vmap(place_rows)(base_w, cycle_pos, cycle_wrows, pair_pos, pair_wrows)
    return migrated.reshape(PARTICLES, S), group_logw.reshape(PARTICLES), mean_state
```

```python
import functools

import jax
import jax.numpy as jnp
from jax import lax
from jax.experimental import pallas as pl
from jax.experimental.pallas import tpu as pltpu
from jax.sharding import PartitionSpec as P

MESH = pl.DeviceIdType.MESH
F32 = jnp.float32
BF16 = jnp.bfloat16
LANES = 128
CHUNK = 256


def column(row_block):
    rows = jnp.broadcast_to(row_block, (8, row_block.shape[1]))
    return rows.T[:, 0:1]


def kernel(
    nb,
    npair,
    part_hbm,
    prior_ref,
    trans_hbm,
    drive_ref,
    cur_ref,
    decay_ref,
    obsm_hbm,
    weight_ref,
    obs_ref,
    anc_ref,
    cyc_ref,
    pair_ref,
    out_ref,
    glw_ref,
    mean_ref,
    state,
    hi,
    lo,
    trans,
    obsm,
    acc,
    pick,
    pick_in,
    rout,
    rin,
    rhi,
    rlo,
    stats,
    load_sem,
    send_sem,
    recv_sem,
    stat_send,
    stat_recv,
):
    n = nb * npair
    b = lax.axis_index("blk")
    p = lax.axis_index("pair")
    me = b * npair + p
    rows, width = state.shape
    blocks = rows // LANES
    steps = obs_ref.shape[0]
    n_cyc = cyc_ref.shape[0] * LANES
    n_pair = pair_ref.shape[1]
    n_in = n_cyc + n_pair
    n_pad = rin.shape[0]

    loads = []
    for c in range(rows // CHUNK):
        part = pl.ds(c * CHUNK, CHUNK)
        loads.append(
            pltpu.make_async_copy(part_hbm.at[part], state.at[part], load_sem.at[c])
        )
    load_t = pltpu.make_async_copy(trans_hbm, trans, load_sem.at[len(loads)])
    load_o = pltpu.make_async_copy(obsm_hbm, obsm, load_sem.at[len(loads) + 1])
    for copy in loads:
        copy.start()
    load_t.start()
    load_o.start()

    barrier = pltpu.get_barrier_semaphore()

    def greet(k, carry):
        other = lax.rem(me + k, n)
        pl.semaphore_signal(
            barrier,
            inc=1,
            device_id=(other // npair, lax.rem(other, npair)),
            device_id_type=MESH,
        )
        return carry

    lax.fori_loop(1, n, greet, 0)

    anc = anc_ref[...].astype(F32)
    picks = [column(cyc_ref[q : q + 1, :].astype(F32)) for q in range(n_cyc // LANES)]
    picks.append(column(pair_ref[...].astype(F32)))
    pick_col = jnp.concatenate(picks, axis=0)
    lane = lax.broadcasted_iota(jnp.int32, (1, LANES), 1).astype(F32)
    place = lax.broadcasted_iota(jnp.int32, (n_in, 1), 0).astype(F32) + float(rows)
    parent = jnp.zeros((n_in, LANES), F32)
    source = []
    for r in range(blocks):
        hit = pick_col == lane + float(r * LANES)
        parent = parent + jnp.where(hit, anc[r : r + 1, :], 0.0)
        moved = jnp.sum(jnp.where(hit, place, 0.0), axis=0, keepdims=True)
        source.append(jnp.where(moved > 0.0, moved, anc[r : r + 1, :]))
    parent = jnp.sum(parent, axis=1, keepdims=True)
    source = jnp.concatenate(source, axis=0)
    wide = lax.broadcasted_iota(jnp.int32, (1, rows), 1).astype(F32)
    take = jnp.where(parent == wide, 1.0, 0.0).astype(BF16)

    sent = jnp.zeros((n_in, width), F32)
    for c, copy in enumerate(loads):
        copy.wait()
        part = slice(c * CHUNK, (c + 1) * CHUNK)
        hi[part, :] = state[part, :].astype(BF16)
        sent = sent + jnp.dot(take[:, part], hi[part, :], preferred_element_type=F32)
    rout[...] = sent

    pl.semaphore_wait(barrier, n - 1)
    right = lax.rem(b + 1, nb)
    across = lax.rem(p + npair // 2, npair)
    half = n_cyc // 2
    spans = [(0, half, (right, p)), (half, half, (right, p)), (n_cyc, n_pair, (b, across))]
    moves = []
    for q, (start, size, target) in enumerate(spans):
        part = pl.ds(start, size)
        move = pltpu.make_async_remote_copy(
            src_ref=rout.at[part],
            dst_ref=rin.at[part],
            send_sem=send_sem.at[q],
            recv_sem=recv_sem.at[q],
            device_id=target,
            device_id_type=MESH,
        )
        move.start()
        moves.append(move)

    load_t.wait()
    load_o.wait()
    decay = decay_ref[...]

    def advance(t, st, h, l, part):
        drift = jnp.dot(h[part, :], trans[...], preferred_element_type=F32)
        drift = drift + cur_ref[t] * drive_ref[...]
        new = decay * st[part, :] + jnp.tanh(drift)
        rounded = new.astype(BF16)
        st[part, :] = new
        h[part, :] = rounded
        if t == steps - 1:
            l[part, :] = (new - rounded.astype(F32)).astype(BF16)
        return rounded

    for t in range(steps):
        for c in range(rows // CHUNK):
            part = slice(c * CHUNK, (c + 1) * CHUNK)
            rounded = advance(t, state, hi, lo, part)
            predicted = jnp.dot(rounded, obsm[...], preferred_element_type=F32)
            misfit = predicted - obs_ref[t : t + 1, :]
            cost = weight_ref[...] * misfit * misfit
            if t:
                cost = cost + acc[part, :]
            acc[part, :] = cost

    prior_t = prior_ref[...].T
    logw = []
    for r in range(blocks):
        part = slice(r * LANES, (r + 1) * LANES)
        logw.append(
            prior_t[:, r : r + 1] - 0.5 * jnp.sum(acc[part, :], axis=1, keepdims=True)
        )
    top = functools.reduce(jnp.maximum, logw)
    top = jnp.max(top, axis=0, keepdims=True)
    mass = jnp.zeros((LANES, 1), F32)
    mean = jnp.zeros((1, width), F32)
    for r in range(blocks):
        part = slice(r * LANES, (r + 1) * LANES)
        expw = jnp.exp(logw[r] - top)
        mass = mass + expw
        mean = mean + jnp.sum(expw * state[part, :], axis=0, keepdims=True)
    mass = jnp.sum(mass, axis=0, keepdims=True)
    cells = [mean[:, q : q + LANES] for q in range(0, width, LANES)]
    cells.append(jnp.broadcast_to(top, (1, LANES)))
    cells += [jnp.broadcast_to(mass, (1, LANES))] * 3
    stats[me] = jnp.concatenate(cells, axis=0)

    def tell(k, carry):
        other = lax.rem(me + k, n)
        pltpu.make_async_remote_copy(
            src_ref=stats.at[me],
            dst_ref=stats.at[me],
            send_sem=stat_send,
            recv_sem=stat_recv,
            device_id=(other // npair, lax.rem(other, npair)),
            device_id_type=MESH,
        ).start()
        return carry

    lax.fori_loop(1, n, tell, 0)

    source_t = source.T
    wide_in = lax.broadcasted_iota(jnp.int32, (1, n_pad), 1).astype(F32) + float(rows)
    for r in range(blocks):
        part = slice(r * LANES, (r + 1) * LANES)
        col = source_t[:, r : r + 1]
        pick[part, :] = jnp.where(col == wide, 1.0, 0.0).astype(BF16)
        pick_in[part, :] = jnp.where(col == wide_in, 1.0, 0.0).astype(BF16)
    for c in range(rows // CHUNK):
        part = slice(c * CHUNK, (c + 1) * CHUNK)
        out_ref[part, :] = jnp.dot(
            pick[part, :], hi[...], preferred_element_type=F32
        ) + jnp.dot(pick[part, :], lo[...], preferred_element_type=F32)

    if n_pad > n_in:
        rhi[n_in:, :] = jnp.zeros((n_pad - n_in, width), BF16)
        rlo[n_in:, :] = jnp.zeros((n_pad - n_in, width), BF16)
    for group in ((0,), (2, 1)):
        parts = []
        for q in group:
            moves[q].wait()
            parts.append(slice(spans[q][0], spans[q][0] + spans[q][1]))
        for part in parts:
            rhi[part, :] = rin[part, :].astype(BF16)
        for t in range(steps):
            for part in parts:
                advance(t, rin, rhi, rlo, part)
    for c in range(rows // CHUNK):
        part = slice(c * CHUNK, (c + 1) * CHUNK)
        out_ref[part, :] += jnp.dot(
            pick_in[part, :], rhi[...], preferred_element_type=F32
        ) + jnp.dot(pick_in[part, :], rlo[...], preferred_element_type=F32)

    others = stats.at[pl.ds(0, n - 1)]
    pltpu.make_async_copy(others, others, stat_send).wait()
    pltpu.make_async_copy(others, others, stat_recv).wait()
    lines = width // LANES
    shares = stats[...]
    tops = shares[:, lines : lines + 1, :]
    peak = jnp.max(tops, axis=0, keepdims=True)
    scaled = jnp.exp(tops - peak) * shares
    summed = jnp.sum(scaled, axis=0)
    total = summed[lines + 1 : lines + 2, :]
    mean_ref[...] = summed[:lines, :] / total

    def group_weight(device):
        share = stats[device]
        part_sum = share[lines + 1 : lines + 2, :] * jnp.exp(
            share[lines : lines + 1, :] - peak[0]
        )
        return jnp.log(jnp.maximum(float(n) * part_sum / total, 0.1))

    own = group_weight(me)
    cyc_w = group_weight(lax.rem(b + nb - 1, nb) * npair + p)
    pair_w = group_weight(b * npair + lax.rem(p + npair - npair // 2, npair))
    glw_ref[...] = jnp.where(
        source < float(rows),
        own,
        jnp.where(source < float(rows + n_cyc), cyc_w, pair_w),
    )


def per_device(nb, npair, *arrays):
    (particles, prior, trans, drive, current, decay, obsm, weight, observed, anc, cyc, pair) = arrays
    rows, width = particles.shape
    n = nb * npair
    n_in = cyc.shape[0] + pair.shape[0]
    n_pad = -(-n_in // LANES) * LANES
    vmem = pl.BlockSpec(memory_space=pltpu.VMEM)
    smem = pl.BlockSpec(memory_space=pltpu.SMEM)
    hbm = pl.BlockSpec(memory_space=pl.ANY)
    migrated, glw, mean = pl.pallas_call(
        functools.partial(kernel, nb, npair),
        out_shape=(
            jax.ShapeDtypeStruct((rows, width), F32),
            jax.ShapeDtypeStruct((rows // LANES, LANES), F32),
            jax.ShapeDtypeStruct((width // LANES, LANES), F32),
        ),
        in_specs=[hbm, vmem, hbm, vmem, smem, vmem, hbm, vmem, vmem, vmem, vmem, vmem],
        out_specs=(vmem, vmem, vmem),
        scratch_shapes=[
            pltpu.VMEM((rows, width), F32),
            pltpu.VMEM((rows, width), BF16),
            pltpu.VMEM((rows, width), BF16),
            pltpu.VMEM(trans.shape, BF16),
            pltpu.VMEM(obsm.shape, BF16),
            pltpu.VMEM((rows, obsm.shape[1]), F32),
            pltpu.VMEM((rows, rows), BF16),
            pltpu.VMEM((rows, n_pad), BF16),
            pltpu.VMEM((n_in, width), F32),
            pltpu.VMEM((n_pad, width), F32),
            pltpu.VMEM((n_pad, width), BF16),
            pltpu.VMEM((n_pad, width), BF16),
            pltpu.VMEM((n, 8, LANES), F32),
            pltpu.SemaphoreType.DMA((rows // CHUNK + 2,)),
            pltpu.SemaphoreType.DMA((3,)),
            pltpu.SemaphoreType.DMA((3,)),
            pltpu.SemaphoreType.DMA,
            pltpu.SemaphoreType.DMA,
        ],
        compiler_params=pltpu.CompilerParams(
            collective_id=0, has_side_effects=True, vmem_limit_bytes=48 * 2**20
        ),
    )(
        particles,
        prior.reshape(rows // LANES, LANES),
        trans,
        drive.reshape(1, width),
        current,
        decay.reshape(1, width),
        obsm,
        weight.reshape(1, -1),
        observed,
        anc.reshape(rows // LANES, LANES),
        cyc.reshape(-1, LANES),
        pair.reshape(1, -1),
    )
    return migrated, glw.reshape(rows), mean.reshape(width)


def solution(mesh):
    shard, rep = P(("blk", "pair")), P()
    rows = P(("blk", "pair"), None)
    return jax.shard_map(
        functools.partial(per_device, mesh.shape["blk"], mesh.shape["pair"]),
        mesh=mesh,
        in_specs=(rows, shard, rep, rep, rep, rep, rep, rep, rep, shard, shard, shard),
        out_specs=(rows, shard, rep),
        check_vma=False,
    )
```

```python
import functools

import jax
import jax.numpy as jnp
from jax import lax
from jax.experimental import pallas as pl
from jax.experimental.pallas import tpu as pltpu
from jax.sharding import PartitionSpec as P

MESH = pl.DeviceIdType.MESH
F32 = jnp.float32
BF16 = jnp.bfloat16
LANES = 128
CHUNK = 256
STEP_CHUNK = 1024
PICK_CHUNK = 512


def column(row_block):
    rows = jnp.broadcast_to(row_block, (8, row_block.shape[1]))
    return rows.T[:, 0:1]


def kernel(
    nb,
    npair,
    part_hbm,
    trans_hbm,
    obsm_hbm,
    anc_hbm,
    cyc_hbm,
    pair_hbm,
    prior_hbm,
    drive_hbm,
    cur_hbm,
    decay_hbm,
    weight_hbm,
    obs_hbm,
    out_ref,
    glw_ref,
    mean_ref,
    state,
    hi,
    trans,
    obsm,
    acc,
    pick,
    pick_in,
    rout,
    rin,
    rhi,
    stats,
    anc_ref,
    cyc_ref,
    pair_ref,
    prior_ref,
    drive_ref,
    cur_ref,
    decay_ref,
    weight_ref,
    obs_ref,
    load_sem,
    small_sem,
    send_sem,
    recv_sem,
    stat_send,
    stat_recv,
):
    n = nb * npair
    b = lax.axis_index("blk")
    p = lax.axis_index("pair")
    me = b * npair + p
    rows, width = state.shape
    blocks = rows // LANES
    steps = obs_ref.shape[0]
    n_cyc = cyc_ref.shape[0] * LANES
    n_pair = pair_ref.shape[1]
    n_in = n_cyc + n_pair
    n_pad = rin.shape[0]

    small = []
    for q, (src, dst) in enumerate(
        (
            (anc_hbm, anc_ref),
            (cyc_hbm, cyc_ref),
            (pair_hbm, pair_ref),
            (prior_hbm, prior_ref),
            (drive_hbm, drive_ref),
            (cur_hbm, cur_ref),
            (decay_hbm, decay_ref),
            (weight_hbm, weight_ref),
            (obs_hbm, obs_ref),
        )
    ):
        small.append(pltpu.make_async_copy(src, dst, small_sem.at[q]))
        small[-1].start()
    loads = []
    for c in range(rows // CHUNK):
        part = pl.ds(c * CHUNK, CHUNK)
        loads.append(
            pltpu.make_async_copy(part_hbm.at[part], state.at[part], load_sem.at[c])
        )
    load_t = pltpu.make_async_copy(trans_hbm, trans, load_sem.at[len(loads)])
    load_o = pltpu.make_async_copy(obsm_hbm, obsm, load_sem.at[len(loads) + 1])
    for copy in loads:
        copy.start()
    load_t.start()
    load_o.start()

    barrier = pltpu.get_barrier_semaphore()

    def greet(k, carry):
        other = lax.rem(me + k, n)
        pl.semaphore_signal(
            barrier,
            inc=1,
            device_id=(other // npair, lax.rem(other, npair)),
            device_id_type=MESH,
        )
        return carry

    lax.fori_loop(1, n, greet, 0)

    for copy in small:
        copy.wait()

    anc = anc_ref[...].astype(F32)
    picks = [column(cyc_ref[q : q + 1, :].astype(F32)) for q in range(n_cyc // LANES)]
    picks.append(column(pair_ref[...].astype(F32)))
    pick_col = jnp.concatenate(picks, axis=0)
    lane = lax.broadcasted_iota(jnp.int32, (1, LANES), 1).astype(F32)
    place = lax.broadcasted_iota(jnp.int32, (n_in, 1), 0).astype(F32) + float(rows)
    parent = jnp.zeros((n_in, LANES), F32)
    source = []
    for r in range(blocks):
        hit = pick_col == lane + float(r * LANES)
        parent = parent + jnp.where(hit, anc[r : r + 1, :], 0.0)
        moved = jnp.sum(jnp.where(hit, place, 0.0), axis=0, keepdims=True)
        source.append(jnp.where(moved > 0.0, moved, anc[r : r + 1, :]))
    parent = jnp.sum(parent, axis=1, keepdims=True)
    source = jnp.concatenate(source, axis=0)
    wide = lax.broadcasted_iota(jnp.int32, (1, rows), 1).astype(F32)
    take = jnp.where(parent == wide, 1.0, 0.0).astype(BF16)

    sent = jnp.zeros((n_in, width), F32)
    for c, copy in enumerate(loads):
        copy.wait()
        part = slice(c * CHUNK, (c + 1) * CHUNK)
        hi[part, :] = state[part, :].astype(BF16)
        sent = sent + jnp.dot(take[:, part], hi[part, :], preferred_element_type=F32)
    rout[...] = sent

    pl.semaphore_wait(barrier, n - 1)
    right = lax.rem(b + 1, nb)
    across = lax.rem(p + npair // 2, npair)
    spans = [(0, n_cyc, (right, p)), (n_cyc, n_pair, (b, across))]
    moves = []
    for q, (start, size, target) in enumerate(spans):
        part = pl.ds(start, size)
        move = pltpu.make_async_remote_copy(
            src_ref=rout.at[part],
            dst_ref=rin.at[part],
            send_sem=send_sem.at[q],
            recv_sem=recv_sem.at[q],
            device_id=target,
            device_id_type=MESH,
        )
        move.start()
        moves.append(move)

    load_t.wait()
    load_o.wait()
    decay = decay_ref[...]

    def advance(t, st, h, part):
        drift = jnp.dot(h[part, :], trans[...], preferred_element_type=F32)
        drift = drift + cur_ref[0:1, t : t + 1] * drive_ref[...]
        new = decay * st[part, :] + jnp.tanh(drift)
        rounded = new.astype(BF16)
        st[part, :] = new
        h[part, :] = rounded
        return rounded

    for t in range(steps):
        for c in range(rows // STEP_CHUNK):
            part = slice(c * STEP_CHUNK, (c + 1) * STEP_CHUNK)
            rounded = advance(t, state, hi, part)
            predicted = jnp.dot(rounded, obsm[...], preferred_element_type=F32)
            misfit = predicted - obs_ref[t : t + 1, :]
            cost = weight_ref[...] * misfit * misfit
            if t:
                cost = cost + acc[part, :]
            acc[part, :] = cost

    prior_t = prior_ref[...].T
    logw = []
    for r in range(blocks):
        part = slice(r * LANES, (r + 1) * LANES)
        logw.append(
            prior_t[:, r : r + 1] - 0.5 * jnp.sum(acc[part, :], axis=1, keepdims=True)
        )
    top = functools.reduce(jnp.maximum, logw)
    top = jnp.max(top, axis=0, keepdims=True)
    mass = jnp.zeros((LANES, 1), F32)
    mean = jnp.zeros((1, width), F32)
    for r in range(blocks):
        part = slice(r * LANES, (r + 1) * LANES)
        expw = jnp.exp(logw[r] - top)
        mass = mass + expw
        mean = mean + jnp.sum(expw * state[part, :], axis=0, keepdims=True)
    mass = jnp.sum(mass, axis=0, keepdims=True)
    cells = [mean[:, q : q + LANES] for q in range(0, width, LANES)]
    cells.append(jnp.broadcast_to(top, (1, LANES)))
    cells += [jnp.broadcast_to(mass, (1, LANES))] * 3
    stats[me] = jnp.concatenate(cells, axis=0)

    def tell(k, carry):
        other = lax.rem(me + k, n)
        pltpu.make_async_remote_copy(
            src_ref=stats.at[me],
            dst_ref=stats.at[me],
            send_sem=stat_send,
            recv_sem=stat_recv,
            device_id=(other // npair, lax.rem(other, npair)),
            device_id_type=MESH,
        ).start()
        return carry

    lax.fori_loop(1, n, tell, 0)

    source_t = source.T
    wide_in = lax.broadcasted_iota(jnp.int32, (1, n_pad), 1).astype(F32) + float(rows)
    for r in range(blocks):
        part = slice(r * LANES, (r + 1) * LANES)
        col = source_t[:, r : r + 1]
        pick[part, :] = jnp.where(col == wide, 1.0, 0.0).astype(BF16)
        pick_in[part, :] = jnp.where(col == wide_in, 1.0, 0.0).astype(BF16)
    if n_pad > n_in:
        rhi[n_in:, :] = jnp.zeros((n_pad - n_in, width), BF16)
    for move in moves:
        move.wait()
    part_in = slice(0, n_in)
    rhi[part_in, :] = rin[part_in, :].astype(BF16)
    for t in range(steps):
        advance(t, rin, rhi, part_in)
    for c in range(rows // PICK_CHUNK):
        part = slice(c * PICK_CHUNK, (c + 1) * PICK_CHUNK)
        out_ref[part, :] = jnp.dot(pick[part, :], hi[...], preferred_element_type=F32)
        out_ref[part, :] += jnp.dot(
            pick_in[part, :], rhi[...], preferred_element_type=F32
        )

    others = stats.at[pl.ds(0, n - 1)]
    pltpu.make_async_copy(others, others, stat_send).wait()
    pltpu.make_async_copy(others, others, stat_recv).wait()
    lines = width // LANES
    shares = stats[...]
    tops = shares[:, lines : lines + 1, :]
    peak = jnp.max(tops, axis=0, keepdims=True)
    scaled = jnp.exp(tops - peak) * shares
    summed = jnp.sum(scaled, axis=0)
    total = summed[lines + 1 : lines + 2, :]
    mean_ref[...] = summed[:lines, :] / total

    def group_weight(device):
        share = stats[device]
        part_sum = share[lines + 1 : lines + 2, :] * jnp.exp(
            share[lines : lines + 1, :] - peak[0]
        )
        return jnp.log(jnp.maximum(float(n) * part_sum / total, 0.1))

    own = group_weight(me)
    cyc_w = group_weight(lax.rem(b + nb - 1, nb) * npair + p)
    pair_w = group_weight(b * npair + lax.rem(p + npair - npair // 2, npair))
    glw_ref[...] = jnp.where(
        source < float(rows),
        own,
        jnp.where(source < float(rows + n_cyc), cyc_w, pair_w),
    )


def per_device(nb, npair, *arrays):
    (particles, prior, trans, drive, current, decay, obsm, weight, observed, anc, cyc, pair) = arrays
    rows, width = particles.shape
    n = nb * npair
    n_in = cyc.shape[0] + pair.shape[0]
    n_pad = -(-n_in // LANES) * LANES
    vmem = pl.BlockSpec(memory_space=pltpu.VMEM)
    hbm = pl.BlockSpec(memory_space=pl.ANY)
    small = (
        anc.reshape(rows // LANES, LANES),
        cyc.reshape(-1, LANES),
        pair.reshape(1, -1),
        prior.reshape(rows // LANES, LANES),
        drive.reshape(1, width),
        current.reshape(1, -1),
        decay.reshape(1, width),
        weight.reshape(1, -1),
        observed,
    )
    migrated, glw, mean = pl.pallas_call(
        functools.partial(kernel, nb, npair),
        out_shape=(
            jax.ShapeDtypeStruct((rows, width), F32),
            jax.ShapeDtypeStruct((rows // LANES, LANES), F32),
            jax.ShapeDtypeStruct((width // LANES, LANES), F32),
        ),
        in_specs=[hbm] * 12,
        out_specs=(vmem, vmem, vmem),
        scratch_shapes=[
            pltpu.VMEM((rows, width), F32),
            pltpu.VMEM((rows, width), BF16),
            pltpu.VMEM(trans.shape, BF16),
            pltpu.VMEM(obsm.shape, BF16),
            pltpu.VMEM((rows, obsm.shape[1]), F32),
            pltpu.VMEM((rows, rows), BF16),
            pltpu.VMEM((rows, n_pad), BF16),
            pltpu.VMEM((n_in, width), F32),
            pltpu.VMEM((n_pad, width), F32),
            pltpu.VMEM((n_pad, width), BF16),
            pltpu.VMEM((n, 8, LANES), F32),
            *[pltpu.VMEM(x.shape, x.dtype) for x in small],
            pltpu.SemaphoreType.DMA((rows // CHUNK + 2,)),
            pltpu.SemaphoreType.DMA((len(small),)),
            pltpu.SemaphoreType.DMA((2,)),
            pltpu.SemaphoreType.DMA((2,)),
            pltpu.SemaphoreType.DMA,
            pltpu.SemaphoreType.DMA,
        ],
        compiler_params=pltpu.CompilerParams(
            collective_id=0, has_side_effects=True, vmem_limit_bytes=64 * 2**20
        ),
    )(particles, trans, obsm, *small)
    migrated, glw, mean = write_out(migrated, glw, mean)
    return migrated, glw.reshape(rows), mean.reshape(width)


def write_kernel(a, b, c, a_out, b_out, c_out):
    a_out[...] = a[...]
    b_out[...] = b[...]
    c_out[...] = c[...]


def write_out(migrated, glw, mean):
    rows, width = migrated.shape
    specs = [
        pl.BlockSpec((CHUNK, width), lambda i: (i, 0)),
        pl.BlockSpec(glw.shape, lambda i: (0, 0)),
        pl.BlockSpec(mean.shape, lambda i: (0, 0)),
    ]
    return pl.pallas_call(
        write_kernel,
        grid=(rows // CHUNK,),
        out_shape=tuple(
            jax.ShapeDtypeStruct(x.shape, x.dtype) for x in (migrated, glw, mean)
        ),
        in_specs=specs,
        out_specs=tuple(specs),
        compiler_params=pltpu.CompilerParams(vmem_limit_bytes=64 * 2**20),
    )(migrated, glw, mean)


def solution(mesh):
    shard, rep = P(("blk", "pair")), P()
    rows = P(("blk", "pair"), None)
    return jax.shard_map(
        functools.partial(per_device, mesh.shape["blk"], mesh.shape["pair"]),
        mesh=mesh,
        in_specs=(rows, shard, rep, rep, rep, rep, rep, rep, rep, shard, shard, shard),
        out_specs=(rows, shard, rep),
        check_vma=False,
    )
```
